256 devices in a mesh: prow: 8 (over x, core), pcol: 32 (over z, y).
Axes of the slice: x: 4, y: 4, z: 8, core: 2. Of those that a mesh axis runs over, the one named last changes fastest.
Arguments:
- anc_mask: int32 [2, 128], P(None, 'prow'), may hold values 0 or 1
- factor: bfloat16 [2, 16384, 2048], P(None, 'prow', 'pcol'), may hold values from -0.046875 to 0.046875
- inverse_block: bfloat16 [16384, 16384], P('prow', 'pcol'), may hold values from -6 to 6
- diag_inverse: float32 [2, 2048, 2048], P(None, 'prow', 'pcol'), may hold values from -6 to 6
Outputs:
- offdiag: float32 [2, 2048, 16384], P(None, 'prow', 'pcol')
- diag_block: float32 [2, 2048, 2048], P(None, 'prow', 'pcol')
The draws below stay inside these ranges and needn't reach their ends.
All inputs are finite; a program needn't handle non-finite values. No bound on the sum of `anc_mask` on one device may be relied on, other than what follows from the above.
Results may differ from the reference program's by a relative error of at most 0.0017.
Values may be sent and summed in bfloat16 or wider, within the bound.
A program may use at most 128 MiB of HBM per device.

```python
import jax
import jax.numpy as jnp

W = 2048
R = 16384
BLK = 128
NBLK = 128


def touch_ends(array, own_key, low, top_value):
    longest = array.shape.index(max(array.shape))
    spots = []
    for shift in (0, 1):
        where = [jax.random.randint(jax.random.fold_in(own_key, axis), (), 0, length) for axis, length in enumerate(array.shape)]
        where[longest] = (where[longest] + shift) % array.shape[longest]
        spots.append(tuple(where))
    return array.at[spots[0]].set(low).at[spots[1]].set(top_value)


def block_scale(key, extent, pieces, low, high):
    def one(axis_at, parts):
        steps = jax.random.uniform(jax.random.fold_in(jax.random.fold_in(key, 6), axis_at), (parts,), jnp.float32, low / len(pieces), high / len(pieces))
        return jnp.repeat(jnp.exp(steps), extent[axis_at] // parts).reshape((-1,) + (1,) * (len(extent) - axis_at - 1))

    gain = one(*pieces[0])
    for cut in pieces[1:]:
        gain = gain * one(*cut)
    return gain


def centred(key, dims, scale, limit, pieces=(), dtype=jnp.bfloat16):
    result = scale * jax.random.normal(key, dims, jnp.float32)
    if pieces:
        result = result * block_scale(key, dims, pieces, -0.22, 0.18)
    return jnp.clip(result, -limit, limit).astype(dtype)


def setup_inputs(seed: int = 0) -> dict:
    key_of = jax.random.split(jax.random.key(seed), 5)
    return {
        "anc_mask": touch_ends((jax.random.randint(key_of[0], (2, NBLK), 0, 4) < 3).astype(jnp.int32), jax.random.fold_in(key_of[0], 1), 0, 1),
        "factor": centred(key_of[1], (2, R, W), R ** -0.5, 0.046875, ((1, 8), (2, 32))),
        "inverse_block": centred(key_of[2], (R, R), 1.0, 6.0, ((0, 8), (1, 32))),
        "diag_inverse": centred(key_of[3], (2, W, W), 1.0, 6.0, ((1, 8), (2, 32)), jnp.float32),
    }


def reference(anc_mask, factor, inverse_block, diag_inverse):
    row_mask = jnp.repeat(anc_mask, BLK, axis=1).astype(jnp.bfloat16)
    masked = factor * row_mask[:, :, None]
    off_list = []
    diag_list = []
    for snode in range(2):
        product = jnp.dot(masked[snode].T, inverse_block, preferred_element_type=jnp.float32)
        off_block = -product
        off_list.append(off_block)
        off_round = off_block.astype(jnp.bfloat16)
        summed = jnp.dot(off_round, masked[snode], preferred_element_type=jnp.float32)
        diag_list.append(diag_inverse[snode] - summed)
    return jnp.stack(off_list), jnp.stack(diag_list)
```

```python
import jax
import jax.numpy as jnp
from jax import lax
from jax.experimental import pallas as pl
from jax.experimental.pallas import tpu as pltpu
from jax.sharding import PartitionSpec as P

MESH = pl.DeviceIdType.MESH
F32 = jnp.float32
BF16 = jnp.bfloat16


def mod(value, size):
    return lax.rem(value + size, size)


def remote(src, dst, send, recv, device):
    return pltpu.make_async_remote_copy(
        src_ref=src, dst_ref=dst, send_sem=send, recv_sem=recv, device_id=device, device_id_type=MESH
    )


def kernel(
    mask_ref, f_ref, b_ref, dinv_ref, off_ref, diag_ref,
    mf, b1, b2, stage, ks, rbuf, xbuf, m2, oq, pt, zbuf, dfin,
    mzs, mzr, mys, myr, pts, ptr, css, csr, xss, xsr, m2xs, m2xr, m2cs, m2cr, m2l, oqs, oqr, zss, zsr, loc,
):
    i = lax.axis_index("prow")
    j = lax.axis_index("pcol")
    x, c = lax.div(i, 2), lax.rem(i, 2)
    z, y = lax.div(j, 4), lax.rem(j, 4)
    a = lax.div(y, 2)
    y1 = y + 1 - 2 * lax.rem(y, 2)
    yp = 3 - y
    y1p = 3 - y1
    slots = (y, y1, yp)

    def dev(x_, c_, z_, y_):
        return (2 * x_ + c_, 4 * z_ + y_)

    mate = dev(x, c, z, yp)
    beside = dev(x, c, z, y1)
    zdev = (dev(x, c, mod(z + 1, 8), y), dev(x, c, mod(z - 1, 8), y))
    sib = dev(x, 1 - c, z, y)

    own_b = pltpu.make_async_copy(b_ref, b1, loc.at[0])
    own_b.start()

    def slot(zb, s, low=0, rows=64):
        return mf.at[zb, pl.ds(pl.multiple_of(64 * s + low, 32), rows)]

    @pl.loop(0, 16)
    def _(b):
        lanes = pl.ds(pl.multiple_of(128 * b, 128), 128)
        keep = mask_ref[a, b].astype(F32)
        mf[z, pl.ds(pl.multiple_of(64 * y, 64), 64), lanes] = (f_ref[a, :, lanes].astype(F32) * keep).astype(BF16)
        other = mask_ref[1 - a, b].astype(F32)
        stage[:, lanes] = (f_ref[1 - a, :, lanes].astype(F32) * other).astype(BF16)

    barrier = pltpu.get_barrier_semaphore()
    greeted = [mate, beside, zdev[0], zdev[1], sib] + [dev(mod(x + k, 4), c, z, y) for k in (1, 2, 3)]
    for device in greeted:
        pl.semaphore_signal(barrier, inc=1, device_id=device, device_id_type=MESH)
    pl.semaphore_wait(barrier, len(greeted))

    def ring(way, t, p, sent):
        sign = 1 if way else -1
        zb = mod(z + sign * (t - 1 if sent else t), 8)
        if t == 4 and p == 2:
            part = slot(zb, slots[2], 32 * way, 32)
        else:
            part = slot(zb, slots[p])
        return remote(part, part, mzs.at[way, t, p], mzr.at[way, t, p], zdev[way])

    ring_steps = [(way, t, p) for t in (1, 2, 3) for p in range(3) for way in (0, 1)]
    ring_steps += [(0, 4, 0), (1, 4, 1), (0, 4, 2), (1, 4, 2)]

    mate_m = remote(stage, slot(z, y), pts.at[0], ptr.at[0], mate)
    mate_b = remote(b_ref, b2, pts.at[1], ptr.at[1], mate)
    beside_a = remote(slot(z, y), slot(z, y), mys.at[8], myr.at[8], beside)

    def beside_b(zb, sent):
        part = slot(zb, yp if sent else y1p)
        return remote(part, part, mys.at[zb], myr.at[zb], beside)

    e = mod(x - lax.div(z, 2), 4)
    col = c == lax.rem(z, 2)
    source = jnp.logical_and(col, e == 0)
    relay = jnp.logical_and(col, e > 0)

    def m2_part(zb, kind):
        return m2.at[zb, pl.ds(pl.multiple_of(64 * kind, 64), 64)]

    def m2_along(zb, kind, first):
        device = dev(mod(x + 1 + 2 * kind, 4), c, z, y)
        src = slot(zb, y + kind * (3 - 2 * y)) if first else m2_part(zb, kind)
        return remote(src, m2_part(zb, kind), m2xs.at[kind, zb], m2xr.at[kind, zb], device)

    def m2_across(zb, kind, first):
        src = slot(zb, y + kind * (3 - 2 * y)) if first else m2_part(zb, kind)
        return remote(src, m2_part(zb, kind), m2cs.at[kind, zb], m2cr.at[kind, zb], sib)

    def m2_here(zb, kind):
        return pltpu.make_async_copy(slot(zb, y + kind * (3 - 2 * y)), m2_part(zb, kind), m2l.at[kind, zb])

    def hops(kind):
        return e + kind * (4 - 2 * e)

    def m2_stage(tau):
        @pl.loop(0, 4)
        def _(q):
            kind, way = lax.div(q, 2), lax.rem(q, 2)
            if tau <= 4:
                fits = jnp.logical_and(tau >= way, tau <= 4 - way)

                @pl.when(jnp.logical_and(source, fits))
                def _():
                    zb = mod(z + (2 * way - 1) * tau, 8)
                    m2_along(zb, kind, True).start()
                    m2_across(zb, kind, True).start()
                    m2_here(zb, kind).start()

            t = tau - hops(kind)
            due = jnp.logical_and(t >= way, t <= 4 - way)

            @pl.when(jnp.logical_and(relay, due))
            def _():
                zb = mod(z + (2 * way - 1) * t, 8)
                m2_along(zb, kind, False).wait_recv()

                @pl.when(hops(kind) < 3)
                def _():
                    m2_along(zb, kind, False).start()

                m2_across(zb, kind, False).start()

    def core_copy(zb, h):
        return remote(ks.at[zb, h], rbuf.at[h, lax.div(zb, 2)], css.at[h, zb], csr.at[h, zb], sib)

    def x_copy(zb, h):
        owner = lax.div(zb, 2)
        place = mod(x - owner, 4) - 1
        return remote(ks.at[zb, h], xbuf.at[place, h], xss.at[h, zb], xsr.at[h, place], dev(owner, c, z, y))

    def unit(zb, h):
        right = (b1, b2)[h]

        @pl.loop(0, 2)
        def _(n):
            lanes = pl.ds(pl.multiple_of(256 * n, 256), 256)
            ks[zb, h, :, lanes] = jnp.dot(mf[zb], right[:, lanes], preferred_element_type=F32)

        @pl.when(lax.rem(zb, 2) != c)
        def _():
            core_copy(zb, h).start()

    def merge(zb, h):
        @pl.when(lax.rem(zb, 2) == c)
        def _():
            core_copy(zb, h).wait_recv()
            ks[zb, h] = ks[zb, h] + rbuf[h, lax.div(zb, 2)]

            @pl.when(lax.div(zb, 2) != x)
            def _():
                x_copy(zb, h).start()

    mate_m.start()
    beside_a.start()
    ring(0, 1, 0, True).start()
    ring(1, 1, 0, True).start()
    mate_b.start()
    beside_a.wait_recv()
    ring(0, 1, 1, True).start()
    ring(1, 1, 1, True).start()
    mate_m.wait_recv()
    ring(0, 1, 2, True).start()
    ring(1, 1, 2, True).start()
    beside_b(z, True).start()
    m2_stage(0)
    own_b.wait()
    beside_b(z, False).wait_recv()
    unit(z, 0)
    merge(z, 0)

    for t in (1, 2, 3):
        near = (mod(z - t, 8), mod(z + t, 8))
        for p in range(3):
            for way in (0, 1):
                ring(way, t, p, False).wait_recv()
                if (way, t + 1, p) in ring_steps:
                    ring(way, t + 1, p, True).start()
                if p == 2:
                    beside_b(near[way], True).start()
        m2_stage(t)
        for zb in near:
            beside_b(zb, False).wait_recv()
            unit(zb, 0)
        for zb in near:
            merge(zb, 0)

    mate_b.wait_recv()

    @pl.loop(0, 7)
    def _(n):
        unit(mod(z + n - 3, 8), 1)

        @pl.when(n > 0)
        def _():
            merge(mod(z + n - 4, 8), 1)

    merge(mod(z + 3, 8), 1)

    far = mod(z + 4, 8)
    for way, t, p in ring_steps[-4:]:
        ring(way, t, p, False).wait_recv()
    beside_b(far, True).start()
    m2_stage(4)
    beside_b(far, False).wait_recv()
    unit(far, 0)
    unit(far, 1)
    merge(far, 0)
    merge(far, 1)
    m2_stage(5)

    def oq_part(s):
        return oq.at[:, pl.ds(pl.multiple_of(512 * s, 512), 512)]

    def oq_copy(h, sent):
        s = ((y, yp) if sent else (y1, y1p))[h]
        return remote(oq_part(s), oq_part(s), oqs.at[h], oqr.at[h], beside)

    off_here = pltpu.make_async_copy(ks.at[i, 0], off_ref.at[a], loc.at[1])
    off_there = remote(ks.at[i, 1], off_ref.at[a], pts.at[2], ptr.at[2], mate)
    for h in (0, 1):
        for place in range(3):
            remote(ks.at[i, h], xbuf.at[place, h], xss.at[h, i], xsr.at[h, place], sib).wait_recv()
        ks[i, h] = -((ks[i, h] + xbuf[0, h]) + (xbuf[1, h] + xbuf[2, h]))
        oq[:, pl.ds(pl.multiple_of(512 * (y, yp)[h], 512), 512)] = ks[i, h].astype(BF16)
        oq_copy(h, True).start()
        (off_here, off_there)[h].start()
    m2_stage(6)
    m2_stage(7)

    @pl.loop(0, 16)
    def _(q):
        zb, kind = lax.div(q, 2), lax.rem(q, 2)

        @pl.when(source)
        def _():
            m2_here(zb, kind).wait()

        @pl.when(jnp.logical_not(col))
        def _():
            m2_across(zb, kind, False).wait_recv()

    for h in (0, 1):
        oq_copy(h, False).wait_recv()

    @pl.loop(0, 8)
    def _(zb):
        pt[zb] = lax.dot_general(m2[zb], oq[...], (((1,), (1,)), ((), ())), preferred_element_type=F32)

    def z_copy(way, k, kind):
        sign = -1 if way else 1
        zb = mod(z + sign * (5 - k), 8)
        return remote(
            pt.at[zb, pl.ds(64 * kind, 64)], zbuf.at[way, k - 1, kind], zss.at[way, k, kind], zsr.at[way, k, kind], zdev[way]
        )

    def z_has(way, k, kind):
        return k > 1 or kind == way

    for k in (1, 2, 3, 4, 5):
        for kind in (0, 1):
            for way in (0, 1):
                if k > 1 and z_has(way, k - 1, kind):
                    z_copy(way, k - 1, kind).wait_recv()
                    zb = mod(z + (-1 if way else 1) * (5 - k), 8)
                    rows = pl.ds(64 * kind, 64)
                    pt[zb, rows] = pt[zb, rows] + zbuf[way, k - 2, kind]
                if k < 5 and z_has(way, k, kind):
                    z_copy(way, k, kind).start()

    last = remote(pt.at[z, pl.ds(64, 64)], dfin, pts.at[3], ptr.at[3], mate)
    last.start()
    diag_ref[a] = dinv_ref[a] - pt[z, pl.ds(0, 64)]
    last.wait_recv()
    diag_ref[1 - a] = dinv_ref[1 - a] - dfin[...]

    last.wait_send()
    off_here.wait()
    off_there.wait_send()
    off_there.wait_recv()
    mate_m.wait_send()
    mate_b.wait_send()
    beside_a.wait_send()
    for way, t, p in ring_steps:
        ring(way, t, p, True).wait_send()
    for h in (0, 1):
        oq_copy(h, True).wait_send()
    for k in (1, 2, 3, 4):
        for kind in (0, 1):
            for way in (0, 1):
                if z_has(way, k, kind):
                    z_copy(way, k, kind).wait_send()

    @pl.loop(0, 8)
    def _(zb):
        beside_b(zb, True).wait_send()
        for h in (0, 1):
            @pl.when(lax.rem(zb, 2) != c)
            def _():
                core_copy(zb, h).wait_send()

            @pl.when(jnp.logical_and(lax.rem(zb, 2) == c, lax.div(zb, 2) != x))
            def _():
                x_copy(zb, h).wait_send()

        for kind in (0, 1):
            @pl.when(col)
            def _():
                m2_across(zb, kind, False).wait_send()

                @pl.when(jnp.logical_or(e == 0, hops(kind) < 3))
                def _():
                    m2_along(zb, kind, False).wait_send()


def shards(anc_mask, factor, inverse_block, diag_inverse):
    vmem = pl.BlockSpec(memory_space=pltpu.VMEM)
    hbm = pl.BlockSpec(memory_space=pl.ANY)
    dma = pltpu.SemaphoreType.DMA
    off, diag = pl.pallas_call(
        kernel,
        out_shape=(jax.ShapeDtypeStruct((2, 256, 512), F32), jax.ShapeDtypeStruct((2, 64, 256), F32)),
        in_specs=[pl.BlockSpec(memory_space=pltpu.SMEM), vmem, hbm, vmem],
        out_specs=(hbm, vmem),
        scratch_shapes=[
            pltpu.VMEM((8, 256, 2048), BF16),
            pltpu.VMEM((2048, 512), BF16),
            pltpu.VMEM((2048, 512), BF16),
            pltpu.VMEM((64, 2048), BF16),
            pltpu.VMEM((8, 2, 256, 512), F32),
            pltpu.VMEM((2, 4, 256, 512), F32),
            pltpu.VMEM((3, 2, 256, 512), F32),
            pltpu.VMEM((8, 128, 2048), BF16),
            pltpu.VMEM((256, 2048), BF16),
            pltpu.VMEM((8, 128, 256), F32),
            pltpu.VMEM((2, 4, 2, 64, 256), F32),
            pltpu.VMEM((64, 256), F32),
            dma((2, 5, 3)), dma((2, 5, 3)),
            dma((9,)), dma((9,)),
            dma((4,)), dma((4,)),
            dma((2, 8)), dma((2, 8)),
            dma((2, 8)), dma((2, 3)),
            dma((2, 8)), dma((2, 8)), dma((2, 8)), dma((2, 8)), dma((2, 8)),
            dma((2,)), dma((2,)),
            dma((2, 5, 2)), dma((2, 5, 2)),
            dma((2,)),
        ],
        compiler_params=pltpu.CompilerParams(
            collective_id=0, has_side_effects=True, vmem_limit_bytes=52 * 2**20
        ),
        cost_estimate=pl.CostEstimate(flops=9663676416, bytes_accessed=2**23, transcendentals=0),
        name="selected_inverse",
    )(anc_mask, factor.transpose(0, 2, 1), inverse_block, diag_inverse.transpose(0, 2, 1))
    return off, diag.transpose(0, 2, 1)


def solution(mesh):
    placed = (P(None, "prow"), P(None, "prow", "pcol"), P("prow", "pcol"), P(None, "prow", "pcol"))
    return jax.shard_map(
        shards,
        mesh=mesh,
        in_specs=placed,
        out_specs=(P(None, "prow", "pcol"), P(None, "prow", "pcol")),
        check_vma=False,
    )
```

```python
import jax
import jax.numpy as jnp
from jax import lax
from jax.experimental import pallas as pl
from jax.experimental.pallas import tpu as pltpu
from jax.sharding import PartitionSpec as P

MESH = pl.DeviceIdType.MESH
F32 = jnp.float32
BF16 = jnp.bfloat16
H = 2
SR = 64 // H
WR = 256 // H


def mod(value, size):
    return lax.rem(value + size, size)


def remote(src, dst, send, recv, device):
    return pltpu.make_async_remote_copy(
        src_ref=src, dst_ref=dst, send_sem=send, recv_sem=recv, device_id=device, device_id_type=MESH
    )


def kernel(
    mask_hbm, f_hbm, b_ref, dinv_hbm, off_ref, diag_ref,
    mask_ref, f_ref, dinv_ref, mf, b1, b2, stage, ks, rbuf, xbuf, hbuf, m2, oq, pt, zbuf, dfin,
    mzs, mzr, mas, mar, mys, myr, mms, mmr, pts, ptr, css, csr, xss, xsr, hsr,
    m2xs, m2xr, m2cs, m2cr, m2l, oqs, oqr, offs, offr, zss, zsr, dfs, dfr, loc,
):
    i = lax.axis_index("prow")
    j = lax.axis_index("pcol")
    x, c = lax.div(i, 2), lax.rem(i, 2)
    z, y = lax.div(j, 4), lax.rem(j, 4)
    a = lax.div(y, 2)
    y1 = y + 1 - 2 * lax.rem(y, 2)
    yp = 3 - y
    y1p = 3 - y1
    slots = (y, y1, yp)

    def dev(x_, c_, z_, y_):
        return (2 * x_ + c_, 4 * z_ + y_)

    mate = dev(x, c, z, yp)
    beside = dev(x, c, z, y1)
    zdev = (dev(x, c, mod(z + 1, 8), y), dev(x, c, mod(z - 1, 8), y))
    xdev = (dev(mod(x + 1, 4), c, z, y), dev(mod(x - 1, 4), c, z, y))
    sib = dev(x, 1 - c, z, y)

    loads = [
        pltpu.make_async_copy(src, dst, loc.at[n])
        for n, (src, dst) in enumerate(((mask_hbm, mask_ref), (f_hbm, f_ref), (b_ref, b1), (dinv_hbm, dinv_ref)))
    ]
    for load in loads:
        load.start()
    barrier = pltpu.get_barrier_semaphore()
    greeted = [mate, beside, zdev[0], zdev[1], xdev[0], xdev[1], sib]
    for device in greeted:
        pl.semaphore_signal(barrier, inc=1, device_id=device, device_id_type=MESH)
    loads[0].wait()
    loads[1].wait()

    @pl.loop(0, 16)
    def _(b):
        lanes = pl.ds(pl.multiple_of(128 * b, 128), 128)
        keep = mask_ref[a, b].astype(F32)
        other = mask_ref[1 - a, b].astype(F32)
        for hf in range(H):
            rows = pl.ds(SR * hf, SR)
            mf[z, hf, y, :, lanes] = (f_ref[a, rows, lanes].astype(F32) * keep).astype(BF16)
            stage[hf, :, lanes] = (f_ref[1 - a, rows, lanes].astype(F32) * other).astype(BF16)

    pl.semaphore_wait(barrier, len(greeted))

    def ring(way, hf, t, p, sent):
        sign = 1 if way else -1
        zb = mod(z + sign * (t - 1 if sent else t), 8)
        part = mf.at[zb, hf, slots[p]]
        if t == 4 and p == 2:
            part = mf.at[zb, hf, slots[2], pl.ds(SR // 2 * way, SR // 2)]
        return remote(part, part, mzs.at[hf, way, t, p], mzr.at[hf, way, t, p], zdev[way])

    near_steps = [(way, t, p) for t in (1, 2, 3) for p in range(3) for way in (0, 1)]
    far_steps = [(0, 4, 0), (1, 4, 1), (0, 4, 2), (1, 4, 2)]
    ring_steps = near_steps + far_steps

    def mate_m(hf):
        return remote(stage.at[hf], mf.at[z, hf, y], mms.at[hf], mmr.at[hf], mate)

    def mate_b(n):
        lanes = pl.ds(256 * n, 256)
        return remote(b_ref.at[:, lanes], b2.at[:, lanes], pts.at[n], ptr.at[n], mate)

    def beside_a(hf):
        return remote(mf.at[z, hf, y], mf.at[z, hf, y], mas.at[hf], mar.at[hf], beside)

    def beside_b(zb, hf, sent):
        part = mf.at[zb, hf, yp if sent else y1p]
        return remote(part, part, mys.at[hf, zb], myr.at[hf, zb], beside)

    e = mod(x - lax.div(z, 2), 4)
    col = c == lax.rem(z, 2)
    source = jnp.logical_and(col, e == 0)
    relay = jnp.logical_and(col, e > 0)

    def m2_part(zb, hf, kind):
        return m2.at[zb, pl.ds(pl.multiple_of(64 * kind + SR * hf, SR), SR)]

    def m2_from(zb, hf, kind, first):
        return mf.at[zb, hf, y + kind * (3 - 2 * y)] if first else m2_part(zb, hf, kind)

    def m2_along(zb, hf, kind, first):
        device = dev(mod(x + 1 + 2 * kind, 4), c, z, y)
        return remote(
            m2_from(zb, hf, kind, first), m2_part(zb, hf, kind), m2xs.at[hf, kind, zb], m2xr.at[hf, kind, zb], device
        )

    def m2_across(zb, hf, kind, first):
        return remote(
            m2_from(zb, hf, kind, first), m2_part(zb, hf, kind), m2cs.at[hf, kind, zb], m2cr.at[hf, kind, zb], sib
        )

    def m2_here(zb, hf, kind):
        return pltpu.make_async_copy(m2_from(zb, hf, kind, True), m2_part(zb, hf, kind), m2l.at[hf, kind, zb])

    def hops(kind):
        return e + kind * (4 - 2 * e)

    def m2_stage(tau):
        @pl.loop(0, 4)
        def _(q):
            kind, way = lax.div(q, 2), lax.rem(q, 2)
            if tau < 5 * H:
                fits = jnp.logical_and(tau % 5 >= way, tau % 5 <= 4 - way)

                @pl.when(jnp.logical_and(source, fits))
                def _():
                    zb = mod(z + (2 * way - 1) * (tau % 5), 8)
                    m2_along(zb, tau // 5, kind, True).start()
                    m2_across(zb, tau // 5, kind, True).start()
                    m2_here(zb, tau // 5, kind).start()

            n = tau - hops(kind)
            t = lax.rem(n + 5, 5)
            due = jnp.logical_and(jnp.logical_and(n >= 0, n < 5 * H), jnp.logical_and(t >= way, t <= 4 - way))

            @pl.when(jnp.logical_and(relay, due))
            def _():
                hf = lax.div(n, 5)
                zb = mod(z + (2 * way - 1) * t, 8)
                m2_along(zb, hf, kind, False).wait_recv()

                @pl.when(hops(kind) < 3)
                def _():
                    m2_along(zb, hf, kind, False).start()

                m2_across(zb, hf, kind, False).start()

    def window(g):
        return (0, 0, 512) if g == 0 else (1, 256 * (g - 1), 256)

    def tile(ref, g, index, rows=pl.ds(0, 4)):
        h, low, width = window(g)
        return ref.at[index + (h, rows, pl.ds(0, SR), pl.ds(low, width))]

    def core_copy(zb, hf, g):
        return remote(
            tile(ks, g, (zb, hf)), tile(rbuf, g, (lax.div(zb, 2), hf)), css.at[hf, g, zb], csr.at[hf, g, zb], sib
        )

    def unit(zb, hf, g):
        h, low, width = window(g)
        left = mf[zb, hf].reshape(WR, 2048)
        right = (b1, b2)[h]
        for at in range(low, low + width, 256):
            lanes = pl.ds(at, 256)
            ks[zb, hf, h, :, :, lanes] = jnp.dot(left, right[:, lanes], preferred_element_type=F32).reshape(4, SR, 256)

        @pl.when(lax.rem(zb, 2) != c)
        def _():
            core_copy(zb, hf, g).start()

    def place(zb, hh):
        return mod((1 - 2 * hh) * (lax.div(zb, 2) - x), 4)

    def x_copy(zb, hf, g, hh, dst, recv, device):
        src = tile(ks, g, (zb, hf), pl.ds(2 * hh, 2))
        h, low, width = window(g)
        return remote(
            src, dst.at[:, :, pl.ds(low, width)], xss.at[hf, g, hh, zb], recv, device
        )

    def x_direct(zb, hf, g, hh):
        return x_copy(zb, hf, g, hh, xbuf.at[hf, window(g)[0], hh, 1], xsr.at[hf, g, hh, 1], xdev[1 - hh])

    def x_first(zb, hf, g, hh):
        return x_copy(zb, hf, g, hh, hbuf.at[hf, window(g)[0], hh], hsr.at[hf, g, hh], xdev[hh])

    def x_second(zb, hf, g, hh):
        return x_copy(zb, hf, g, hh, xbuf.at[hf, window(g)[0], hh, 0], xsr.at[hf, g, hh, 0], xdev[hh])

    def merge(zb, hf, g):
        h, low, width = window(g)
        lanes = pl.ds(low, width)

        @pl.when(lax.rem(zb, 2) == c)
        def _():
            core_copy(zb, hf, g).wait_recv()
            ks[zb, hf, h, :, :, lanes] = ks[zb, hf, h, :, :, lanes] + rbuf[lax.div(zb, 2), hf, h, :, :, lanes]
            for hh in (0, 1):
                @pl.when(place(zb, hh) == 2)
                def _():
                    x_first(zb, hf, g, hh).start()

                @pl.when(place(zb, hh) == 3)
                def _():
                    x_direct(zb, hf, g, hh).start()

    def pass_on(zb, hf, g):
        h, low, width = window(g)
        lanes = pl.ds(low, width)
        for hh in (0, 1):
            @pl.when(jnp.logical_and(lax.rem(zb, 2) == c, place(zb, hh) == 1))
            def _():
                x_first(zb, hf, g, hh).wait_recv()
                rows = pl.ds(2 * hh, 2)
                ks[zb, hf, h, rows, :, lanes] = ks[zb, hf, h, rows, :, lanes] + hbuf[hf, h, hh, :, :, lanes]
                x_second(zb, hf, g, hh).start()

    for hf in range(H):
        mate_m(hf).start()
        beside_a(hf).start()
        if hf == 0:
            ring(0, 0, 1, 0, True).start()
            ring(1, 0, 1, 0, True).start()
    mate_b(0).start()
    mate_b(1).start()
    beside_a(0).wait_recv()
    ring(0, 0, 1, 1, True).start()
    ring(1, 0, 1, 1, True).start()
    mate_m(0).wait_recv()
    ring(0, 0, 1, 2, True).start()
    ring(1, 0, 1, 2, True).start()
    beside_b(z, 0, True).start()
    loads[2].wait()

    def blocks(t):
        return (z,) if t == 0 else (far,) if t == 4 else (mod(z - t, 8), mod(z + t, 8))

    far = mod(z + 4, 8)

    def arrived(hf, t):
        for zb in blocks(t):
            beside_b(zb, hf, False).wait_recv()

    def many(first, count, hf, g, *works):
        for work in works:
            @pl.loop(0, count)
            def _(n):
                work(mod(z + first + n, 8), hf, g)

    def each(hf, t, g, *works):
        for work in works:
            for zb in blocks(t):
                work(zb, hf, g)

    def do(f, *rest):
        return lambda: f(*rest)

    fill = {}

    def put(hf, t, p, f, *rest):
        fill.setdefault((hf, t, p), []).append(do(f, *rest))

    for hf in range(H):
        for t in (0, 1, 2, 3):
            put(hf, t + 1, 1, arrived, hf, t)
            put(hf, t + 1, 1, each, hf, t, 0, unit)
            put(hf, t + 1, 2, each, hf, t, 0, merge)
            if t < 3:
                put(hf, t + 2, 0, each, hf, t, 0, pass_on)
    put(1, 1, 0, each, 0, 3, 0, pass_on)
    put(1, 1, 0, arrived, 0, 4)
    put(1, 1, 0, each, 0, 4, 0, unit)
    put(1, 1, 1, each, 0, 4, 0, merge)
    put(1, 1, 1, mate_b(0).wait_recv)
    put(1, 1, 2, many, -1, 3, 0, 1, unit, merge)
    put(1, 2, 0, each, 0, 4, 0, pass_on)
    put(1, 2, 1, many, -1, 3, 0, 1, pass_on)
    put(1, 2, 1, many, 2, 5, 0, 1, unit)
    put(1, 2, 2, many, 2, 5, 0, 1, merge)
    put(1, 3, 0, many, 2, 5, 0, 1, pass_on)
    put(1, 3, 1, many, -1, 3, 1, 1, unit)
    put(1, 3, 2, many, -1, 3, 1, 1, merge)
    put(1, 4, 0, many, -1, 3, 1, 1, pass_on)

    for hf in range(H):
        for t in (1, 2, 3, 4):
            for p in range(3):
                for way in (0, 1):
                    if (way, t, p) in ring_steps:
                        ring(way, hf, t, p, False).wait_recv()
                    if (way, t + 1, p) in ring_steps:
                        ring(way, hf, t + 1, p, True).start()
                    if p == 2 and t < 4:
                        beside_b(blocks(t)[way], hf, True).start()
                if p == 2 and t == 4:
                    beside_b(far, hf, True).start()
                if t == 3 and hf + 1 < H:
                    if p == 1:
                        beside_a(hf + 1).wait_recv()
                    if p == 2:
                        mate_m(hf + 1).wait_recv()
                        beside_b(z, hf + 1, True).start()
                    for way in (0, 1):
                        ring(way, hf + 1, 1, p, True).start()
                for work in fill.get((hf, t, p), ()):
                    work()
                if p == 1 and t == 1 and hf == 0:
                    m2_stage(0)
                if p == 2:
                    m2_stage(5 * hf + t)
                    if t == 4 and hf + 1 < H:
                        m2_stage(5 * (hf + 1))

    def oq_part(hf, s):
        return oq.at[hf, :, pl.ds(pl.multiple_of(512 * s, 512), 512)]

    def oq_copy(hf, h, sent):
        s = ((y, yp) if sent else (y1, y1p))[h]
        return remote(oq_part(hf, s), oq_part(hf, s), oqs.at[hf, h], oqr.at[hf, h], beside)

    def off_here(hf):
        return pltpu.make_async_copy(ks.at[i, hf, 0], off_ref.at[a, :, hf], offs.at[hf, 0])

    def off_there(hf):
        return remote(ks.at[i, hf, 1], off_ref.at[a, :, hf], offs.at[hf, 1], offr.at[hf], mate)

    def finish(hf, h):
        for hh in (0, 1):
            for g in (0,) if h == 0 else (1, 2):
                x_direct(i, hf, g, hh).wait_recv()
                x_second(i, hf, g, hh).wait_recv()
            rows = pl.ds(2 * hh, 2)
            ks[i, hf, h, rows] = -((ks[i, hf, h, rows] + xbuf[hf, h, hh, 0]) + xbuf[hf, h, hh, 1])
        s = (y, yp)[h]
        oq[hf, :, pl.ds(pl.multiple_of(512 * s, 512), 512)] = ks[i, hf, h].reshape(WR, 512).astype(BF16)
        oq_copy(hf, h, True).start()
        (off_here, off_there)[h](hf).start()

    def second(hf):
        for h in (0, 1):
            oq_copy(hf, h, False).wait_recv()

        @pl.loop(0, 8)
        def _(zb):
            pt[hf, zb] = lax.dot_general(m2[zb], oq[hf], (((1,), (1,)), ((), ())), preferred_element_type=F32)

    def z_copy(hf, way, k, kind):
        zb = mod(z + (-1 if way else 1) * (5 - k), 8)
        return remote(
            pt.at[hf, zb, pl.ds(64 * kind, 64)], zbuf.at[hf, way, k - 1, kind],
            zss.at[hf, way, k, kind], zsr.at[hf, way, k, kind], zdev[way],
        )

    def z_has(way, k, kind):
        return k > 1 or kind == way

    def z_sum(hf, k):
        for kind in (0, 1):
            for way in (0, 1):
                if k > 1 and z_has(way, k - 1, kind):
                    z_copy(hf, way, k - 1, kind).wait_recv()
                    zb = mod(z + (-1 if way else 1) * (5 - k), 8)
                    rows = pl.ds(64 * kind, 64)
                    pt[hf, zb, rows] = pt[hf, zb, rows] + zbuf[hf, way, k - 2, kind]
                if k < 5 and z_has(way, k, kind):
                    z_copy(hf, way, k, kind).start()

    def dfin_copy(hf):
        return remote(pt.at[hf, z, pl.ds(64, 64)], dfin.at[hf], dfs.at[hf], dfr.at[hf], mate)

    def drain():
        mate_b(0).wait_send()
        mate_b(1).wait_send()
        for hf in range(H):
            mate_m(hf).wait_send()
            beside_a(hf).wait_send()
            for way, t, p in ring_steps:
                ring(way, hf, t, p, True).wait_send()

        @pl.loop(0, 8)
        def _(zb):
            for hf in range(H):
                beside_b(zb, hf, True).wait_send()
                for g in range(3):
                    @pl.when(lax.rem(zb, 2) != c)
                    def _():
                        core_copy(zb, hf, g).wait_send()

                    @pl.when(jnp.logical_and(lax.rem(zb, 2) == c, lax.div(zb, 2) != x))
                    def _():
                        for hh in (0, 1):
                            x_first(zb, hf, g, hh).wait_send()

                for kind in (0, 1):
                    @pl.when(col)
                    def _():
                        m2_across(zb, hf, kind, False).wait_send()

                        @pl.when(jnp.logical_or(e == 0, hops(kind) < 3))
                        def _():
                            m2_along(zb, hf, kind, False).wait_send()

    finish(0, 0)
    mate_b(1).wait_recv()
    many(0, 8, 0, 2, unit, merge)
    each(1, 3, 0, pass_on)
    arrived(1, 4)
    each(1, 4, 0, unit)
    many(2, 5, 1, 1, unit)
    each(1, 4, 0, merge)
    many(0, 8, 0, 2, pass_on)
    many(2, 5, 1, 1, merge)
    m2_stage(5 * H)
    many(0, 8, 1, 2, unit)
    finish(0, 1)
    many(0, 8, 1, 2, merge)
    each(1, 4, 0, pass_on)
    many(2, 5, 1, 1, pass_on)
    m2_stage(5 * H + 1)
    many(0, 8, 1, 2, pass_on)
    m2_stage(5 * H + 2)
    finish(1, 0)

    @pl.loop(0, 16)
    def _(q):
        zb, kind = lax.div(q, 2), lax.rem(q, 2)
        for hf in range(H):
            @pl.when(source)
            def _():
                m2_here(zb, hf, kind).wait()

            @pl.when(jnp.logical_not(col))
            def _():
                m2_across(zb, hf, kind, False).wait_recv()

    second(0)
    z_sum(0, 1)
    finish(1, 1)
    z_sum(0, 2)
    z_sum(0, 3)
    second(1)
    z_sum(1, 1)
    z_sum(0, 4)
    z_sum(1, 2)
    z_sum(0, 5)
    dfin_copy(0).start()
    z_sum(1, 3)
    drain()
    z_sum(1, 4)
    z_sum(1, 5)
    dfin_copy(1).start()

    def lanes_in_order(parts):
        return jnp.concatenate([parts[hf][:, SR * s : SR * (s + 1)] for s in range(4) for hf in range(H)], axis=1)

    loads[3].wait()
    diag_ref[a] = dinv_ref[a] - lanes_in_order([pt[hf, z, pl.ds(0, 64)] for hf in range(H)])
    for hf in range(H):
        dfin_copy(hf).wait_recv()
    diag_ref[1 - a] = dinv_ref[1 - a] - lanes_in_order([dfin[hf] for hf in range(H)])

    for hf in range(H):
        dfin_copy(hf).wait_send()
        off_here(hf).wait()
        off_there(hf).wait()
        for h in (0, 1):
            oq_copy(hf, h, True).wait_send()
        for k in (1, 2, 3, 4):
            for kind in (0, 1):
                for way in (0, 1):
                    if z_has(way, k, kind):
                        z_copy(hf, way, k, kind).wait_send()


def shards(anc_mask, factor, inverse_block, diag_inverse):
    vmem = pl.BlockSpec(memory_space=pltpu.VMEM)
    hbm = pl.BlockSpec(memory_space=pl.ANY)
    dma = pltpu.SemaphoreType.DMA
    off, diag = pl.pallas_call(
        kernel,
        out_shape=(jax.ShapeDtypeStruct((2, 4, H, SR, 512), F32), jax.ShapeDtypeStruct((2, 64, 256), F32)),
        in_specs=[hbm, hbm, hbm, hbm],
        out_specs=(hbm, vmem),
        scratch_shapes=[
            pltpu.SMEM((2, 16), jnp.int32),
            pltpu.VMEM((2, 64, 2048), BF16),
            pltpu.VMEM((2, 64, 256), F32),
            pltpu.VMEM((8, H, 4, SR, 2048), BF16),
            pltpu.VMEM((2048, 512), BF16),
            pltpu.VMEM((2048, 512), BF16),
            pltpu.VMEM((H, SR, 2048), BF16),
            pltpu.VMEM((8, H, 2, 4, SR, 512), F32),
            pltpu.VMEM((4, H, 2, 4, SR, 512), F32),
            pltpu.VMEM((H, 2, 2, 2, 2, SR, 512), F32),
            pltpu.VMEM((H, 2, 2, 2, SR, 512), F32),
            pltpu.VMEM((8, 128, 2048), BF16),
            pltpu.VMEM((H, WR, 2048), BF16),
            pltpu.VMEM((H, 8, 128, WR), F32),
            pltpu.VMEM((H, 2, 4, 2, 64, WR), F32),
            pltpu.VMEM((H, 64, WR), F32),
            dma((H, 2, 5, 3)), dma((H, 2, 5, 3)),
            dma((H,)), dma((H,)),
            dma((H, 8)), dma((H, 8)),
            dma((H,)), dma((H,)),
            dma((2,)), dma((2,)),
            dma((H, 3, 8)), dma((H, 3, 8)),
            dma((H, 3, 2, 8)), dma((H, 3, 2, 2)), dma((H, 3, 2)),
            dma((H, 2, 8)), dma((H, 2, 8)), dma((H, 2, 8)), dma((H, 2, 8)), dma((H, 2, 8)),
            dma((H, 2)), dma((H, 2)),
            dma((H, 2)), dma((H,)),
            dma((H, 2, 5, 2)), dma((H, 2, 5, 2)),
            dma((H,)), dma((H,)),
            dma((4,)),
        ],
        compiler_params=pltpu.CompilerParams(
            collective_id=0, has_side_effects=True, vmem_limit_bytes=62 * 2**20
        ),
        cost_estimate=pl.CostEstimate(flops=9663676416, bytes_accessed=2**23, transcendentals=0),
        name="selected_inverse",
    )(anc_mask, factor.transpose(0, 2, 1), inverse_block, diag_inverse.transpose(0, 2, 1))
    return off.reshape(2, 256, 512), diag.transpose(0, 2, 1)


def solution(mesh):
    placed = (P(None, "prow"), P(None, "prow", "pcol"), P("prow", "pcol"), P(None, "prow", "pcol"))
    return jax.shard_map(
        shards,
        mesh=mesh,
        in_specs=placed,
        out_specs=(P(None, "prow", "pcol"), P(None, "prow", "pcol")),
        check_vma=False,
    )
```

```python
import jax
import jax.numpy as jnp
from jax import lax
from jax.experimental import pallas as pl
from jax.experimental.pallas import tpu as pltpu
from jax.sharding import PartitionSpec as P

MESH = pl.DeviceIdType.MESH
F32 = jnp.float32
BF16 = jnp.bfloat16
H = 1
LAG = 2
SR = 64 // H
WR = 256 // H


def mod(value, size):
    return lax.rem(value + size, size)


def remote(src, dst, send, recv, device):
    return pltpu.make_async_remote_copy(
        src_ref=src, dst_ref=dst, send_sem=send, recv_sem=recv, device_id=device, device_id_type=MESH
    )


def kernel(
    mask_hbm, f_hbm, b_ref, dinv_hbm, off_ref, diag_ref,
    mask_ref, f_ref, dinv_ref, mf, b1, b2, stage, ks, rbuf, xbuf, hbuf, m2, oq, pt, zbuf, dfin,
    mzs, mzr, mas, mar, mys, myr, mms, mmr, pts, ptr, css, csr, xss, xsr, hsr,
    m2xs, m2xr, m2cs, m2cr, m2l, oqs, oqr, offs, offr, zss, zsr, dfs, dfr, loc,
):
    i = lax.axis_index("prow")
    j = lax.axis_index("pcol")
    x, c = lax.div(i, 2), lax.rem(i, 2)
    z, y = lax.div(j, 4), lax.rem(j, 4)
    a = lax.div(y, 2)
    y1 = y + 1 - 2 * lax.rem(y, 2)
    yp = 3 - y
    y1p = 3 - y1
    slots = (y, yp, y1)

    def dev(x_, c_, z_, y_):
        return (2 * x_ + c_, 4 * z_ + y_)

    mate = dev(x, c, z, yp)
    beside = dev(x, c, z, y1)
    zdev = (dev(x, c, mod(z + 1, 8), y), dev(x, c, mod(z - 1, 8), y))
    xdev = (dev(mod(x + 1, 4), c, z, y), dev(mod(x - 1, 4), c, z, y))
    sib = dev(x, 1 - c, z, y)

    loads = [
        pltpu.make_async_copy(src, dst, loc.at[n])
        for n, (src, dst) in enumerate(((mask_hbm, mask_ref), (f_hbm, f_ref), (b_ref, b1), (dinv_hbm, dinv_ref)))
    ]
    for load in loads:
        load.start()
    barrier = pltpu.get_barrier_semaphore()
    across = (dev(x, c, mod(z + 1, 8), yp), dev(x, c, mod(z - 1, 8), yp))
    greeted = [mate, beside, zdev[0], zdev[1], xdev[0], xdev[1], sib, across[0], across[1]]
    for device in greeted:
        pl.semaphore_signal(barrier, inc=1, device_id=device, device_id_type=MESH)
    loads[0].wait()
    loads[1].wait()

    @pl.loop(0, 16)
    def _(b):
        lanes = pl.ds(pl.multiple_of(128 * b, 128), 128)
        keep = mask_ref[a, b].astype(F32)
        other = mask_ref[1 - a, b].astype(F32)
        for hf in range(H):
            rows = pl.ds(SR * hf, SR)
            mf[z, hf, y, :, lanes] = (f_ref[a, rows, lanes].astype(F32) * keep).astype(BF16)
            stage[hf, :, lanes] = (f_ref[1 - a, rows, lanes].astype(F32) * other).astype(BF16)

    pl.semaphore_wait(barrier, len(greeted))

    def ring(way, hf, t, p, sent):
        sign = 1 if way else -1
        zb = mod(z + sign * (t - 1 if sent else t), 8)
        part = mf.at[zb, hf, slots[p]]
        if t == 4 and p == 1:
            part = mf.at[zb, hf, slots[1], pl.ds(SR // 2 * way, SR // 2)]
        return remote(part, part, mzs.at[hf, way, t, p], mzr.at[hf, way, t, p], zdev[way])

    near_steps = [(way, t, p) for t in (1, 2, 3) for p in range(3) for way in (0, 1)]
    far_steps = [(0, 4, 0), (0, 4, 1), (1, 4, 1), (1, 4, 2)]
    ring_steps = near_steps + far_steps

    def mate_m(hf):
        return remote(stage.at[hf], mf.at[z, hf, y], mms.at[hf], mmr.at[hf], mate)

    def mate_b(n):
        _, low, width = window(n + 1)
        lanes = pl.ds(low, width)
        return remote(b_ref.at[:, lanes], b2.at[:, lanes], pts.at[n], ptr.at[n], mate)

    def beside_a(hf):
        return remote(mf.at[z, hf, y], mf.at[z, hf, y], mas.at[hf], mar.at[hf], beside)

    def beside_b(zb, hf, sent):
        part = mf.at[zb, hf, yp if sent else y1p]
        return remote(part, part, mys.at[hf, zb], myr.at[hf, zb], beside)

    e = mod(x - lax.div(z, 2), 4)
    col = c == lax.rem(z, 2)
    source = jnp.logical_and(col, e == 0)
    relay = jnp.logical_and(col, e > 0)

    def m2_part(zb, hf, kind):
        return m2.at[zb, pl.ds(pl.multiple_of(64 * kind + SR * hf, SR), SR)]

    def m2_from(zb, hf, kind, first):
        return mf.at[zb, hf, y + kind * (3 - 2 * y)] if first else m2_part(zb, hf, kind)

    def m2_along(zb, hf, kind, first):
        device = dev(mod(x + 1 + 2 * kind, 4), c, z, y)
        return remote(
            m2_from(zb, hf, kind, first), m2_part(zb, hf, kind), m2xs.at[hf, kind, zb], m2xr.at[hf, kind, zb], device
        )

    def m2_across(zb, hf, kind, first):
        return remote(
            m2_from(zb, hf, kind, first), m2_part(zb, hf, kind), m2cs.at[hf, kind, zb], m2cr.at[hf, kind, zb], sib
        )

    def m2_here(zb, hf, kind):
        return pltpu.make_async_copy(m2_from(zb, hf, kind, True), m2_part(zb, hf, kind), m2l.at[hf, kind, zb])

    def hops(kind):
        return e + kind * (4 - 2 * e)

    def m2_stage(sigma):
        @pl.loop(0, 4)
        def _(q):
            kind, way = lax.div(q, 2), lax.rem(q, 2)
            if sigma % 3 == 2 and sigma <= 14:
                step = sigma // 3
                fits = jnp.logical_and(step >= way, step <= 4 - way)

                @pl.when(jnp.logical_and(source, fits))
                def _():
                    zb = mod(z + (2 * way - 1) * step, 8)
                    m2_along(zb, 0, kind, True).start()
                    m2_across(zb, 0, kind, True).start()
                    m2_here(zb, 0, kind).start()

            n = sigma - 2 - LAG * hops(kind)
            t = lax.div(n, 3)
            whole = jnp.logical_and(n >= 0, lax.rem(n, 3) == 0)
            due = jnp.logical_and(whole, jnp.logical_and(t >= way, t <= 4 - way))

            @pl.when(jnp.logical_and(relay, due))
            def _():
                zb = mod(z + (2 * way - 1) * t, 8)
                m2_along(zb, 0, kind, False).wait_recv()

                @pl.when(hops(kind) < 3)
                def _():
                    m2_along(zb, 0, kind, False).start()

                m2_across(zb, 0, kind, False).start()

    def window(g):
        return ((0, 0, 512), (1, 0, 256), (1, 256, 128), (1, 384, 128))[g]

    def tile(ref, g, index, rows=pl.ds(0, 4)):
        h, low, width = window(g)
        return ref.at[index + (h, rows, pl.ds(0, SR), pl.ds(low, width))]

    def core_copy(zb, hf, g):
        return remote(
            tile(ks, g, (zb, hf)), tile(rbuf, g, (lax.div(zb, 2), hf)), css.at[hf, g, zb], csr.at[hf, g, zb], sib
        )

    def unit(zb, hf, g):
        h, low, width = window(g)
        left = mf[zb, hf].reshape(WR, 2048)
        right = (b1, b2)[h]
        step = min(width, 256)

        @pl.loop(0, width // step)
        def _(n):
            lanes = pl.ds(pl.multiple_of(low + step * n, step), step)
            ks[zb, hf, h, :, :, lanes] = jnp.dot(left, right[:, lanes], preferred_element_type=F32).reshape(4, SR, step)

        @pl.when(lax.rem(zb, 2) != c)
        def _():
            core_copy(zb, hf, g).start()

    def place(zb, hh):
        return mod((1 - 2 * hh) * (lax.div(zb, 2) - x), 4)

    def x_copy(zb, hf, g, hh, dst, recv, device):
        src = tile(ks, g, (zb, hf), pl.ds(2 * hh, 2))
        h, low, width = window(g)
        return remote(
            src, dst.at[:, :, pl.ds(low, width)], xss.at[hf, g, hh, zb], recv, device
        )

    def x_direct(zb, hf, g, hh):
        return x_copy(zb, hf, g, hh, xbuf.at[hf, window(g)[0], hh, 1], xsr.at[hf, g, hh, 1], xdev[1 - hh])

    def x_first(zb, hf, g, hh):
        return x_copy(zb, hf, g, hh, hbuf.at[hf, window(g)[0], hh], hsr.at[hf, g, hh], xdev[hh])

    def x_second(zb, hf, g, hh):
        return x_copy(zb, hf, g, hh, xbuf.at[hf, window(g)[0], hh, 0], xsr.at[hf, g, hh, 0], xdev[hh])

    def merge(zb, hf, g):
        h, low, width = window(g)
        lanes = pl.ds(low, width)

        @pl.when(lax.rem(zb, 2) == c)
        def _():
            core_copy(zb, hf, g).wait_recv()
            ks[zb, hf, h, :, :, lanes] = ks[zb, hf, h, :, :, lanes] + rbuf[lax.div(zb, 2), hf, h, :, :, lanes]
            for hh in (0, 1):
                @pl.when(place(zb, hh) == 2)
                def _():
                    x_first(zb, hf, g, hh).start()

                @pl.when(place(zb, hh) == 3)
                def _():
                    x_direct(zb, hf, g, hh).start()

    def pass_on(zb, hf, g):
        h, low, width = window(g)
        lanes = pl.ds(low, width)
        for hh in (0, 1):
            @pl.when(jnp.logical_and(lax.rem(zb, 2) == c, place(zb, hh) == 1))
            def _():
                x_first(zb, hf, g, hh).wait_recv()
                rows = pl.ds(2 * hh, 2)
                ks[zb, hf, h, rows, :, lanes] = ks[zb, hf, h, rows, :, lanes] + hbuf[hf, h, hh, :, :, lanes]
                x_second(zb, hf, g, hh).start()

    for hf in range(H):
        mate_m(hf).start()
        beside_a(hf).start()
        if hf == 0:
            ring(0, 0, 1, 0, True).start()
            ring(1, 0, 1, 0, True).start()
    for n in range(3):
        mate_b(n).start()
    mate_m(0).wait_recv()
    ring(0, 0, 1, 1, True).start()
    ring(1, 0, 1, 1, True).start()
    beside_b(z, 0, True).start()
    beside_a(0).wait_recv()
    ring(0, 0, 1, 2, True).start()
    ring(1, 0, 1, 2, True).start()
    loads[2].wait()

    def blocks(t):
        return (z,) if t == 0 else (far,) if t == 4 else (mod(z - t, 8), mod(z + t, 8))

    far = mod(z + 4, 8)

    def one(zb, *works):
        for work, *rest in works:
            work(zb, 0, *rest)

    def arrive(zb, hf):
        beside_b(zb, hf, False).wait_recv()

    def many(first, count, hf, g, work):
        @pl.loop(0, count)
        def _(n):
            work(mod(z + first + n, 8), hf, g)

    def do(f, *rest):
        return lambda: f(*rest)

    fill = {}

    def put(hf, t, p, f, *rest):
        fill.setdefault((hf, t, p), []).append(do(f, *rest))

    put(0, 1, 0, one, z, (arrive,), (unit, 0))
    put(0, 1, 1, one, z, (merge, 0))
    put(0, 1, 2, one, z, (pass_on, 0))
    for t in (1, 2, 3):
        low, high = blocks(t)
        extra = ((), (1,), (1, 2))[t - 1]
        put(0, t + 1, 0, one, low, (arrive,), (unit, 0), *[(unit, g) for g in extra])
        put(0, t + 1, 1, one, low, (merge, 0), *[(merge, g) for g in extra])
        put(0, t + 1, 1, one, high, (arrive,), (unit, 0), *[(unit, g) for g in extra])
        put(0, t + 1, 2, one, high, (merge, 0), *[(merge, g) for g in extra])
        put(0, t + 1, 2, one, low, (pass_on, 0), *[(pass_on, g) for g in extra])
        if t < 3:
            put(0, t + 2, 0, one, high, (pass_on, 0), *[(pass_on, g) for g in extra])
    put(0, 2, 2, mate_b(0).wait_recv)
    put(0, 2, 2, many, -1, 3, 0, 1, unit)
    put(0, 3, 0, many, -1, 3, 0, 1, merge)
    put(0, 3, 2, many, -1, 3, 0, 1, pass_on)
    put(0, 3, 2, mate_b(1).wait_recv)
    put(0, 3, 2, many, -2, 5, 0, 2, unit)
    put(0, 4, 0, many, -2, 5, 0, 2, merge)
    put(0, 4, 2, many, -2, 5, 0, 2, pass_on)
    put(0, 4, 2, mate_b(2).wait_recv)
    put(0, 4, 2, many, -3, 7, 0, 3, unit)

    m2_stage(2)
    for hf in range(H):
        for t in (1, 2, 3, 4):
            for p in range(3):
                for way in (0, 1):
                    if (way, t, p) in ring_steps:
                        ring(way, hf, t, p, False).wait_recv()
                    if (way, t + 1, p) in ring_steps:
                        ring(way, hf, t + 1, p, True).start()
                    if p == 1 and t < 4:
                        beside_b(blocks(t)[way], hf, True).start()
                if p == 1 and t == 4:
                    beside_b(far, hf, True).start()
                if t == 3 and hf + 1 < H:
                    if p == 1:
                        beside_a(hf + 1).wait_recv()
                    if p == 2:
                        mate_m(hf + 1).wait_recv()
                        beside_b(z, hf + 1, True).start()
                    for way in (0, 1):
                        ring(way, hf + 1, 1, p, True).start()
                for work in fill.get((hf, t, p), ()):
                    work()
                m2_stage(3 * t + p)

    def oq_part(hf, s):
        return oq.at[hf, pl.ds(pl.multiple_of(512 * s, 512), 512)]

    def oq_copy(hf, h, sent):
        s = ((y, yp) if sent else (y1, y1p))[h]
        return remote(oq_part(hf, s), oq_part(hf, s), oqs.at[hf, h], oqr.at[hf, h], beside)

    def off_here(hf):
        return pltpu.make_async_copy(ks.at[i, hf, 0], off_ref.at[a, :, hf], offs.at[hf, 0])

    def off_there(hf):
        return remote(ks.at[i, hf, 1], off_ref.at[a, :, hf], offs.at[hf, 1], offr.at[hf], mate)

    def finish(hf, h):
        for hh in (0, 1):
            for g in (0,) if h == 0 else (1, 2, 3):
                x_direct(i, hf, g, hh).wait_recv()
                x_second(i, hf, g, hh).wait_recv()
            rows = pl.ds(2 * hh, 2)
            ks[i, hf, h, rows] = -((ks[i, hf, h, rows] + xbuf[hf, h, hh, 0]) + xbuf[hf, h, hh, 1])
        s = (y, yp)[h]
        oq[hf, pl.ds(pl.multiple_of(512 * s, 512), 512)] = ks[i, hf, h].reshape(WR, 512).T.astype(BF16)
        oq_copy(hf, h, True).start()
        (off_here, off_there)[h](hf).start()

    def swapped(hf):
        for h in (0, 1):
            oq_copy(hf, h, False).wait_recv()

    def second(hf, zb):
        pt[hf, zb] = jnp.dot(m2[zb], oq[hf], preferred_element_type=F32)

    def z_copy(hf, way, k, kind):
        zb = mod(z + (-1 if way else 1) * (5 - k), 8)
        part = pt.at[hf, zb, pl.ds(64 * kind, 64)]
        if k == 4 and kind == 1:
            return remote(part, dfin.at[hf, way], dfs.at[hf, way], dfr.at[hf, way], across[way])
        return remote(
            part, zbuf.at[hf, way, k - 1, kind], zss.at[hf, way, k, kind], zsr.at[hf, way, k, kind], zdev[way]
        )

    def dfin_copy(hf):
        return remote(pt.at[hf, z, pl.ds(64, 64)], dfin.at[hf, 2], dfs.at[hf, 2], dfr.at[hf, 2], mate)

    def z_has(way, k, kind):
        return k > 1 or kind == way

    def z_sum(hf, k):
        if k == 1:
            second(hf, far)
        if 1 < k < 5:
            @pl.loop(0, 2)
            def _(way):
                second(hf, mod(z + (1 - 2 * way) * (5 - k), 8))
        if k == 3:
            second(hf, z)
            dfin_copy(hf).start()
        for kind in (0, 1):
            for way in (0, 1):
                if k > 1 and z_has(way, k - 1, kind) and not (k == 5 and kind == 1):
                    z_copy(hf, way, k - 1, kind).wait_recv()
                    zb = mod(z + (-1 if way else 1) * (5 - k), 8)
                    rows = pl.ds(64 * kind, 64)
                    pt[hf, zb, rows] = pt[hf, zb, rows] + zbuf[hf, way, k - 2, kind]
                if k < 5 and z_has(way, k, kind):
                    z_copy(hf, way, k, kind).start()

    def drain():
        for n in range(3):
            mate_b(n).wait_send()
        for hf in range(H):
            mate_m(hf).wait_send()
            beside_a(hf).wait_send()
            for way, t, p in ring_steps:
                ring(way, hf, t, p, True).wait_send()

        @pl.loop(0, 8)
        def _(zb):
            for hf in range(H):
                beside_b(zb, hf, True).wait_send()
                for g in range(4):
                    @pl.when(lax.rem(zb, 2) != c)
                    def _():
                        core_copy(zb, hf, g).wait_send()

                    @pl.when(jnp.logical_and(lax.rem(zb, 2) == c, lax.div(zb, 2) != x))
                    def _():
                        for hh in (0, 1):
                            x_first(zb, hf, g, hh).wait_send()

                for kind in (0, 1):
                    @pl.when(col)
                    def _():
                        m2_across(zb, hf, kind, False).wait_send()

                        @pl.when(jnp.logical_or(e == 0, hops(kind) < 3))
                        def _():
                            m2_along(zb, hf, kind, False).wait_send()

    arrive(far, 0)
    for g in range(4):
        unit(far, 0, g)
    m2_stage(15)
    m2_stage(16)
    many(-3, 7, 0, 3, merge)
    for g in range(4):
        merge(far, 0, g)
    for g in (0, 1, 2):
        pass_on(blocks(3)[1], 0, g)
    many(-3, 7, 0, 3, pass_on)
    m2_stage(17)
    for g in range(4):
        pass_on(far, 0, g)
    finish(0, 0)
    m2_stage(18)
    finish(0, 1)
    m2_stage(20)
    drain()

    @pl.loop(0, 16)
    def _(q):
        zb, kind = lax.div(q, 2), lax.rem(q, 2)
        for hf in range(H):
            @pl.when(source)
            def _():
                m2_here(zb, hf, kind).wait()

            @pl.when(jnp.logical_not(col))
            def _():
                m2_across(zb, hf, kind, False).wait_recv()

    swapped(0)
    for k in (1, 2, 3, 4, 5):
        z_sum(0, k)

    def lanes_in_order(parts):
        return jnp.concatenate([parts[hf][:, SR * s : SR * (s + 1)] for s in range(4) for hf in range(H)], axis=1)

    loads[3].wait()
    diag_ref[a] = dinv_ref[a] - lanes_in_order([pt[hf, z, pl.ds(0, 64)] for hf in range(H)])
    for hf in range(H):
        z_copy(hf, 0, 4, 1).wait_recv()
        z_copy(hf, 1, 4, 1).wait_recv()
        dfin_copy(hf).wait_recv()
    diag_ref[1 - a] = dinv_ref[1 - a] - lanes_in_order(
        [(dfin[hf, 0] + dfin[hf, 1]) + dfin[hf, 2] for hf in range(H)]
    )

    for hf in range(H):
        dfin_copy(hf).wait_send()
        off_here(hf).wait()
        off_there(hf).wait()
        for h in (0, 1):
            oq_copy(hf, h, True).wait_send()
        for k in (1, 2, 3, 4):
            for kind in (0, 1):
                for way in (0, 1):
                    if z_has(way, k, kind):
                        z_copy(hf, way, k, kind).wait_send()


def shards(anc_mask, factor, inverse_block, diag_inverse):
    vmem = pl.BlockSpec(memory_space=pltpu.VMEM)
    hbm = pl.BlockSpec(memory_space=pl.ANY)
    dma = pltpu.SemaphoreType.DMA
    off, diag = pl.pallas_call(
        kernel,
        out_shape=(jax.ShapeDtypeStruct((2, 4, H, SR, 512), F32), jax.ShapeDtypeStruct((2, 64, 256), F32)),
        in_specs=[hbm, hbm, hbm, hbm],
        out_specs=(hbm, vmem),
        scratch_shapes=[
            pltpu.SMEM((2, 16), jnp.int32),
            pltpu.VMEM((2, 64, 2048), BF16),
            pltpu.VMEM((2, 64, 256), F32),
            pltpu.VMEM((8, H, 4, SR, 2048), BF16),
            pltpu.VMEM((2048, 512), BF16),
            pltpu.VMEM((2048, 512), BF16),
            pltpu.VMEM((H, SR, 2048), BF16),
            pltpu.VMEM((8, H, 2, 4, SR, 512), F32),
            pltpu.VMEM((4, H, 2, 4, SR, 512), F32),
            pltpu.VMEM((H, 2, 2, 2, 2, SR, 512), F32),
            pltpu.VMEM((H, 2, 2, 2, SR, 512), F32),
            pltpu.VMEM((8, 128, 2048), BF16),
            pltpu.VMEM((H, 2048, WR), BF16),
            pltpu.VMEM((H, 8, 128, WR), F32),
            pltpu.VMEM((H, 2, 4, 2, 64, WR), F32),
            pltpu.VMEM((H, 3, 64, WR), F32),
            dma((H, 2, 5, 3)), dma((H, 2, 5, 3)),
            dma((H,)), dma((H,)),
            dma((H, 8)), dma((H, 8)),
            dma((H,)), dma((H,)),
            dma((3,)), dma((3,)),
            dma((H, 4, 8)), dma((H, 4, 8)),
            dma((H, 4, 2, 8)), dma((H, 4, 2, 2)), dma((H, 4, 2)),
            dma((H, 2, 8)), dma((H, 2, 8)), dma((H, 2, 8)), dma((H, 2, 8)), dma((H, 2, 8)),
            dma((H, 2)), dma((H, 2)),
            dma((H, 2)), dma((H,)),
            dma((H, 2, 5, 2)), dma((H, 2, 5, 2)),
            dma((H, 3)), dma((H, 3)),
            dma((4,)),
        ],
        compiler_params=pltpu.CompilerParams(
            collective_id=0, has_side_effects=True, vmem_limit_bytes=58 * 2**20
        ),
        cost_estimate=pl.CostEstimate(flops=9663676416, bytes_accessed=2**23, transcendentals=0),
        name="selected_inverse",
    )(anc_mask, factor.transpose(0, 2, 1), inverse_block, diag_inverse.transpose(0, 2, 1))
    return off.reshape(2, 256, 512), diag.transpose(0, 2, 1)


def solution(mesh):
    placed = (P(None, "prow"), P(None, "prow", "pcol"), P("prow", "pcol"), P(None, "prow", "pcol"))
    return jax.shard_map(
        shards,
        mesh=mesh,
        in_specs=placed,
        out_specs=(P(None, "prow", "pcol"), P(None, "prow", "pcol")),
        check_vma=False,
    )
```

```python
import jax
import jax.numpy as jnp
from jax import lax
from jax.experimental import pallas as pl
from jax.experimental.pallas import tpu as pltpu
from jax.sharding import PartitionSpec as P

MESH = pl.DeviceIdType.MESH
F32 = jnp.float32
BF16 = jnp.bfloat16
H = 1
LAG = 2
SR = 64 // H
WR = 256 // H


def mod(value, size):
    return lax.rem(value + size, size)


def remote(src, dst, send, recv, device):
    return pltpu.make_async_remote_copy(
        src_ref=src, dst_ref=dst, send_sem=send, recv_sem=recv, device_id=device, device_id_type=MESH
    )


def kernel(
    mask_hbm, f_hbm, b_ref, dinv_hbm, off_ref, diag_ref,
    mask_ref, f_ref, dinv_ref, mf, b1, b2, stage, ks, rbuf, xbuf, hbuf, m2, oq, pt, zbuf, dfin,
    mzs, mzr, mas, mar, mys, myr, mms, mmr, pts, ptr, css, csr, xss, xsr, hsr,
    m2xs, m2xr, m2cs, m2cr, m2l, oqs, oqr, offs, offr, zss, zsr, dfs, dfr, loc,
):
    i = lax.axis_index("prow")
    j = lax.axis_index("pcol")
    x, c = lax.div(i, 2), lax.rem(i, 2)
    z, y = lax.div(j, 4), lax.rem(j, 4)
    a = lax.div(y, 2)
    y1 = y + 1 - 2 * lax.rem(y, 2)
    yp = 3 - y
    y1p = 3 - y1
    slots = (y, yp, y1)

    def dev(x_, c_, z_, y_):
        return (2 * x_ + c_, 4 * z_ + y_)

    mate = dev(x, c, z, yp)
    beside = dev(x, c, z, y1)
    zdev = (dev(x, c, mod(z + 1, 8), y), dev(x, c, mod(z - 1, 8), y))
    xdev = (dev(mod(x + 1, 4), c, z, y), dev(mod(x - 1, 4), c, z, y))
    sib = dev(x, 1 - c, z, y)

    loads = [
        pltpu.make_async_copy(src, dst, loc.at[n])
        for n, (src, dst) in enumerate(((mask_hbm, mask_ref), (f_hbm, f_ref), (b_ref, b1), (dinv_hbm, dinv_ref)))
    ]
    for load in loads:
        load.start()
    barrier = pltpu.get_barrier_semaphore()
    across = (dev(x, c, mod(z + 1, 8), yp), dev(x, c, mod(z - 1, 8), yp))
    greeted = [mate, beside, zdev[0], zdev[1], xdev[0], xdev[1], sib, across[0], across[1]]
    for device in greeted:
        pl.semaphore_signal(barrier, inc=1, device_id=device, device_id_type=MESH)
    loads[0].wait()
    loads[1].wait()

    @pl.loop(0, 16)
    def _(b):
        lanes = pl.ds(pl.multiple_of(128 * b, 128), 128)
        keep = mask_ref[a, b].astype(F32)
        other = mask_ref[1 - a, b].astype(F32)
        for hf in range(H):
            rows = pl.ds(SR * hf, SR)
            mf[z, hf, y, :, lanes] = (f_ref[a, rows, lanes].astype(F32) * keep).astype(BF16)
            stage[hf, :, lanes] = (f_ref[1 - a, rows, lanes].astype(F32) * other).astype(BF16)

    pl.semaphore_wait(barrier, len(greeted))

    def ring(way, hf, t, p, sent):
        sign = 1 if way else -1
        zb = mod(z + sign * (t - 1 if sent else t), 8)
        part = mf.at[zb, hf, slots[p]]
        if t == 4 and p == 1:
            part = mf.at[zb, hf, slots[1], pl.ds(SR // 2 * way, SR // 2)]
        return remote(part, part, mzs.at[hf, way, t, p], mzr.at[hf, way, t, p], zdev[way])

    near_steps = [(way, t, p) for t in (1, 2, 3) for p in range(3) for way in (0, 1)]
    far_steps = [(0, 4, 0), (0, 4, 1), (1, 4, 1), (1, 4, 2)]
    ring_steps = near_steps + far_steps

    def mate_m(hf):
        return remote(stage.at[hf], mf.at[z, hf, y], mms.at[hf], mmr.at[hf], mate)

    def mate_b(n):
        _, low, width = window(n + 1)
        lanes = pl.ds(low, width)
        return remote(b_ref.at[:, lanes], b2.at[:, lanes], pts.at[n], ptr.at[n], mate)

    def beside_a(hf):
        return remote(mf.at[z, hf, y], mf.at[z, hf, y], mas.at[hf], mar.at[hf], beside)

    def beside_b(zb, hf, sent):
        part = mf.at[zb, hf, yp if sent else y1p]
        return remote(part, part, mys.at[hf, zb], myr.at[hf, zb], beside)

    e = mod(x - lax.div(z, 2), 4)
    col = c == lax.rem(z, 2)
    source = jnp.logical_and(col, e == 0)
    relay = jnp.logical_and(col, e > 0)

    def m2_part(zb, hf, kind):
        return m2.at[zb, pl.ds(pl.multiple_of(64 * kind + SR * hf, SR), SR)]

    def m2_from(zb, hf, kind, first):
        return mf.at[zb, hf, y + kind * (3 - 2 * y)] if first else m2_part(zb, hf, kind)

    def m2_along(zb, hf, kind, first):
        device = dev(mod(x + 1 + 2 * kind, 4), c, z, y)
        return remote(
            m2_from(zb, hf, kind, first), m2_part(zb, hf, kind), m2xs.at[hf, kind, zb], m2xr.at[hf, kind, zb], device
        )

    def m2_across(zb, hf, kind, first):
        return remote(
            m2_from(zb, hf, kind, first), m2_part(zb, hf, kind), m2cs.at[hf, kind, zb], m2cr.at[hf, kind, zb], sib
        )

    def m2_here(zb, hf, kind):
        return pltpu.make_async_copy(m2_from(zb, hf, kind, True), m2_part(zb, hf, kind), m2l.at[hf, kind, zb])

    def hops(kind):
        return e + kind * (4 - 2 * e)

    def m2_stage(sigma):
        @pl.loop(0, 4)
        def _(q):
            kind, way = lax.div(q, 2), lax.rem(q, 2)
            if sigma % 3 == 2 and sigma <= 14:
                step = sigma // 3
                fits = jnp.logical_and(step >= way, step <= 4 - way)

                @pl.when(jnp.logical_and(source, fits))
                def _():
                    zb = mod(z + (2 * way - 1) * step, 8)
                    m2_along(zb, 0, kind, True).start()
                    m2_across(zb, 0, kind, True).start()
                    m2_here(zb, 0, kind).start()

            n = sigma - 2 - LAG * hops(kind)
            t = lax.div(n, 3)
            whole = jnp.logical_and(n >= 0, lax.rem(n, 3) == 0)
            due = jnp.logical_and(whole, jnp.logical_and(t >= way, t <= 4 - way))

            @pl.when(jnp.logical_and(relay, due))
            def _():
                zb = mod(z + (2 * way - 1) * t, 8)
                m2_along(zb, 0, kind, False).wait_recv()

                @pl.when(hops(kind) < 3)
                def _():
                    m2_along(zb, 0, kind, False).start()

                m2_across(zb, 0, kind, False).start()

    def window(g):
        return ((0, 0, 512), (1, 0, 256), (1, 256, 128), (1, 384, 128))[g]

    def tile(ref, g, index, rows=pl.ds(0, 4)):
        h, low, width = window(g)
        return ref.at[index + (h, rows, pl.ds(0, SR), pl.ds(low, width))]

    def core_copy(zb, hf, g):
        return remote(
            tile(ks, g, (zb, hf)), tile(rbuf, g, (lax.div(zb, 2), hf)), css.at[hf, g, zb], csr.at[hf, g, zb], sib
        )

    def unit(zb, hf, g):
        h, low, width = window(g)
        left = mf[zb, hf].reshape(WR, 2048)
        right = (b1, b2)[h]
        step = min(width, 256)

        @pl.loop(0, width // step)
        def _(n):
            lanes = pl.ds(pl.multiple_of(low + step * n, step), step)
            ks[zb, hf, h, :, :, lanes] = jnp.dot(left, right[:, lanes], preferred_element_type=F32).reshape(4, SR, step)

        @pl.when(lax.rem(zb, 2) != c)
        def _():
            core_copy(zb, hf, g).start()

    def place(zb, hh):
        return mod((1 - 2 * hh) * (lax.div(zb, 2) - x), 4)

    def x_copy(zb, hf, g, hh, dst, recv, device):
        src = tile(ks, g, (zb, hf), pl.ds(2 * hh, 2))
        h, low, width = window(g)
        return remote(
            src, dst.at[:, :, pl.ds(low, width)], xss.at[hf, g, hh, zb], recv, device
        )

    def x_direct(zb, hf, g, hh):
        return x_copy(zb, hf, g, hh, xbuf.at[hf, window(g)[0], hh, 1], xsr.at[hf, g, hh, 1], xdev[1 - hh])

    def x_first(zb, hf, g, hh):
        return x_copy(zb, hf, g, hh, hbuf.at[hf, window(g)[0], hh], hsr.at[hf, g, hh], xdev[hh])

    def x_second(zb, hf, g, hh):
        return x_copy(zb, hf, g, hh, xbuf.at[hf, window(g)[0], hh, 0], xsr.at[hf, g, hh, 0], xdev[hh])

    def merge(zb, hf, g):
        h, low, width = window(g)
        lanes = pl.ds(low, width)

        @pl.when(lax.rem(zb, 2) == c)
        def _():
            core_copy(zb, hf, g).wait_recv()
            ks[zb, hf, h, :, :, lanes] = ks[zb, hf, h, :, :, lanes] + rbuf[lax.div(zb, 2), hf, h, :, :, lanes]
            for hh in (0, 1):
                @pl.when(place(zb, hh) == 2)
                def _():
                    x_first(zb, hf, g, hh).start()

                @pl.when(place(zb, hh) == 3)
                def _():
                    x_direct(zb, hf, g, hh).start()

    def pass_on(zb, hf, g):
        h, low, width = window(g)
        lanes = pl.ds(low, width)
        for hh in (0, 1):
            @pl.when(jnp.logical_and(lax.rem(zb, 2) == c, place(zb, hh) == 1))
            def _():
                x_first(zb, hf, g, hh).wait_recv()
                rows = pl.ds(2 * hh, 2)
                ks[zb, hf, h, rows, :, lanes] = ks[zb, hf, h, rows, :, lanes] + hbuf[hf, h, hh, :, :, lanes]
                x_second(zb, hf, g, hh).start()

    for hf in range(H):
        mate_m(hf).start()
        beside_a(hf).start()
        if hf == 0:
            ring(0, 0, 1, 0, True).start()
            ring(1, 0, 1, 0, True).start()
    for n in range(3):
        mate_b(n).start()
    mate_m(0).wait_recv()
    ring(0, 0, 1, 1, True).start()
    ring(1, 0, 1, 1, True).start()
    beside_b(z, 0, True).start()
    beside_a(0).wait_recv()
    ring(0, 0, 1, 2, True).start()
    ring(1, 0, 1, 2, True).start()
    loads[2].wait()

    def blocks(t):
        return (z,) if t == 0 else (far,) if t == 4 else (mod(z - t, 8), mod(z + t, 8))

    far = mod(z + 4, 8)

    def one(zb, *works):
        for work, *rest in works:
            work(zb, 0, *rest)

    def arrive(zb, hf):
        beside_b(zb, hf, False).wait_recv()

    def many(first, count, hf, g, work):
        @pl.loop(0, count)
        def _(n):
            work(mod(z + first + n, 8), hf, g)

    def do(f, *rest):
        return lambda: f(*rest)

    fill = {}

    def put(hf, t, p, f, *rest):
        fill.setdefault((hf, t, p), []).append(do(f, *rest))

    put(0, 1, 0, one, z, (arrive,), (unit, 0))
    put(0, 1, 1, one, z, (merge, 0))
    put(0, 1, 2, one, z, (pass_on, 0))
    put(0, 2, 2, mate_b(0).wait_recv)
    put(0, 2, 2, many, -1, 3, 0, 1, unit)
    put(0, 3, 0, many, -1, 3, 0, 1, merge)
    for t in (1, 2, 3):
        low, high = blocks(t)
        extra = ((), (1,), (1, 2))[t - 1]
        put(0, t, 2, one, low, (arrive,), (unit, 0), *[(unit, g) for g in extra])
        put(0, t + 1, 0, one, low, (merge, 0), *[(merge, g) for g in extra])
        put(0, t + 1, 0, one, high, (arrive,), (unit, 0), *[(unit, g) for g in extra])
        put(0, t + 1, 1, one, high, (merge, 0), *[(merge, g) for g in extra])
        put(0, t + 1, 1, one, low, (pass_on, 0), *[(pass_on, g) for g in extra])
        put(0, t + 1, 2, one, high, (pass_on, 0), *[(pass_on, g) for g in extra])
    put(0, 3, 1, many, -1, 3, 0, 1, pass_on)
    put(0, 3, 1, mate_b(1).wait_recv)
    put(0, 3, 1, many, -2, 5, 0, 2, unit)
    fill[(0, 3, 2)].insert(0, do(many, -2, 5, 0, 2, merge))
    put(0, 4, 1, many, -2, 5, 0, 2, pass_on)
    put(0, 4, 2, mate_b(2).wait_recv)
    put(0, 4, 2, many, -3, 7, 0, 3, unit)

    m2_stage(2)
    for hf in range(H):
        for t in (1, 2, 3, 4):
            for p in range(3):
                for way in (0, 1):
                    if (way, t, p) in ring_steps:
                        ring(way, hf, t, p, False).wait_recv()
                    if (way, t + 1, p) in ring_steps:
                        ring(way, hf, t + 1, p, True).start()
                    if p == 1 and t < 4:
                        beside_b(blocks(t)[way], hf, True).start()
                if p == 1 and t == 4:
                    beside_b(far, hf, True).start()
                if t == 3 and hf + 1 < H:
                    if p == 1:
                        beside_a(hf + 1).wait_recv()
                    if p == 2:
                        mate_m(hf + 1).wait_recv()
                        beside_b(z, hf + 1, True).start()
                    for way in (0, 1):
                        ring(way, hf + 1, 1, p, True).start()
                for work in fill.get((hf, t, p), ()):
                    work()
                m2_stage(3 * t + p)

    def oq_part(hf, s):
        return oq.at[hf, pl.ds(pl.multiple_of(512 * s, 512), 512)]

    def oq_copy(hf, h, sent):
        s = ((y, yp) if sent else (y1, y1p))[h]
        return remote(oq_part(hf, s), oq_part(hf, s), oqs.at[hf, h], oqr.at[hf, h], beside)

    def off_here(hf):
        return pltpu.make_async_copy(ks.at[i, hf, 0], off_ref.at[a, :, hf], offs.at[hf, 0])

    def off_there(hf):
        return remote(ks.at[i, hf, 1], off_ref.at[a, :, hf], offs.at[hf, 1], offr.at[hf], mate)

    def finish(hf, h):
        for hh in (0, 1):
            for g in (0,) if h == 0 else (1, 2, 3):
                x_direct(i, hf, g, hh).wait_recv()
                x_second(i, hf, g, hh).wait_recv()
            rows = pl.ds(2 * hh, 2)
            ks[i, hf, h, rows] = -((ks[i, hf, h, rows] + xbuf[hf, h, hh, 0]) + xbuf[hf, h, hh, 1])
        s = (y, yp)[h]
        oq[hf, pl.ds(pl.multiple_of(512 * s, 512), 512)] = ks[i, hf, h].reshape(WR, 512).T.astype(BF16)
        oq_copy(hf, h, True).start()
        (off_here, off_there)[h](hf).start()

    def swapped(hf):
        for h in (0, 1):
            oq_copy(hf, h, False).wait_recv()

    def second(hf, zb):
        pt[hf, zb] = jnp.dot(m2[zb], oq[hf], preferred_element_type=F32)

    def z_copy(hf, way, k, kind):
        zb = mod(z + (-1 if way else 1) * (5 - k), 8)
        part = pt.at[hf, zb, pl.ds(64 * kind, 64)]
        if k == 4 and kind == 1:
            return remote(part, dfin.at[hf, way], dfs.at[hf, way], dfr.at[hf, way], across[way])
        return remote(
            part, zbuf.at[hf, way, k - 1, kind], zss.at[hf, way, k, kind], zsr.at[hf, way, k, kind], zdev[way]
        )

    def dfin_copy(hf):
        return remote(pt.at[hf, z, pl.ds(64, 64)], dfin.at[hf, 2], dfs.at[hf, 2], dfr.at[hf, 2], mate)

    def z_has(way, k, kind):
        return k > 1 or kind == way

    def z_sum(hf, k):
        if k == 1:
            second(hf, far)
        if 1 < k < 5:
            @pl.loop(0, 2)
            def _(way):
                second(hf, mod(z + (1 - 2 * way) * (5 - k), 8))
        if k == 3:
            second(hf, z)
            dfin_copy(hf).start()
        for kind in (0, 1):
            for way in (0, 1):
                if k > 1 and z_has(way, k - 1, kind) and not (k == 5 and kind == 1):
                    z_copy(hf, way, k - 1, kind).wait_recv()
                    zb = mod(z + (-1 if way else 1) * (5 - k), 8)
                    rows = pl.ds(64 * kind, 64)
                    pt[hf, zb, rows] = pt[hf, zb, rows] + zbuf[hf, way, k - 2, kind]
                if k < 5 and z_has(way, k, kind):
                    z_copy(hf, way, k, kind).start()

    def drain():
        for n in range(3):
            mate_b(n).wait_send()
        for hf in range(H):
            mate_m(hf).wait_send()
            beside_a(hf).wait_send()
            for way, t, p in ring_steps:
                ring(way, hf, t, p, True).wait_send()

        @pl.loop(0, 8)
        def _(zb):
            for hf in range(H):
                beside_b(zb, hf, True).wait_send()
                for g in range(4):
                    @pl.when(lax.rem(zb, 2) != c)
                    def _():
                        core_copy(zb, hf, g).wait_send()

                    @pl.when(jnp.logical_and(lax.rem(zb, 2) == c, lax.div(zb, 2) != x))
                    def _():
                        for hh in (0, 1):
                            x_first(zb, hf, g, hh).wait_send()

                for kind in (0, 1):
                    @pl.when(col)
                    def _():
                        m2_across(zb, hf, kind, False).wait_send()

                        @pl.when(jnp.logical_or(e == 0, hops(kind) < 3))
                        def _():
                            m2_along(zb, hf, kind, False).wait_send()

    arrive(far, 0)
    for g in range(4):
        unit(far, 0, g)
    m2_stage(15)
    m2_stage(16)
    many(-3, 7, 0, 3, merge)
    for g in range(4):
        merge(far, 0, g)
    many(-3, 7, 0, 3, pass_on)
    m2_stage(17)
    for g in range(4):
        pass_on(far, 0, g)
    finish(0, 0)
    m2_stage(18)
    finish(0, 1)
    m2_stage(20)
    drain()

    @pl.loop(0, 16)
    def _(q):
        zb, kind = lax.div(q, 2), lax.rem(q, 2)
        for hf in range(H):
            @pl.when(source)
            def _():
                m2_here(zb, hf, kind).wait()

            @pl.when(jnp.logical_not(col))
            def _():
                m2_across(zb, hf, kind, False).wait_recv()

    swapped(0)
    for k in (1, 2, 3, 4, 5):
        z_sum(0, k)

    def lanes_in_order(parts):
        return jnp.concatenate([parts[hf][:, SR * s : SR * (s + 1)] for s in range(4) for hf in range(H)], axis=1)

    loads[3].wait()
    diag_ref[a] = dinv_ref[a] - lanes_in_order([pt[hf, z, pl.ds(0, 64)] for hf in range(H)])
    for hf in range(H):
        z_copy(hf, 0, 4, 1).wait_recv()
        z_copy(hf, 1, 4, 1).wait_recv()
        dfin_copy(hf).wait_recv()
    diag_ref[1 - a] = dinv_ref[1 - a] - lanes_in_order(
        [(dfin[hf, 0] + dfin[hf, 1]) + dfin[hf, 2] for hf in range(H)]
    )

    for hf in range(H):
        dfin_copy(hf).wait_send()
        off_here(hf).wait()
        off_there(hf).wait()
        for h in (0, 1):
            oq_copy(hf, h, True).wait_send()
        for k in (1, 2, 3, 4):
            for kind in (0, 1):
                for way in (0, 1):
                    if z_has(way, k, kind):
                        z_copy(hf, way, k, kind).wait_send()


def shards(anc_mask, factor, inverse_block, diag_inverse):
    vmem = pl.BlockSpec(memory_space=pltpu.VMEM)
    hbm = pl.BlockSpec(memory_space=pl.ANY)
    dma = pltpu.SemaphoreType.DMA
    off, diag = pl.pallas_call(
        kernel,
        out_shape=(jax.ShapeDtypeStruct((2, 4, H, SR, 512), F32), jax.ShapeDtypeStruct((2, 64, 256), F32)),
        in_specs=[hbm, hbm, hbm, hbm],
        out_specs=(hbm, vmem),
        scratch_shapes=[
            pltpu.SMEM((2, 16), jnp.int32),
            pltpu.VMEM((2, 64, 2048), BF16),
            pltpu.VMEM((2, 64, 256), F32),
            pltpu.VMEM((8, H, 4, SR, 2048), BF16),
            pltpu.VMEM((2048, 512), BF16),
            pltpu.VMEM((2048, 512), BF16),
            pltpu.VMEM((H, SR, 2048), BF16),
            pltpu.VMEM((8, H, 2, 4, SR, 512), F32),
            pltpu.VMEM((4, H, 2, 4, SR, 512), F32),
            pltpu.VMEM((H, 2, 2, 2, 2, SR, 512), F32),
            pltpu.VMEM((H, 2, 2, 2, SR, 512), F32),
            pltpu.VMEM((8, 128, 2048), BF16),
            pltpu.VMEM((H, 2048, WR), BF16),
            pltpu.VMEM((H, 8, 128, WR), F32),
            pltpu.VMEM((H, 2, 4, 2, 64, WR), F32),
            pltpu.VMEM((H, 3, 64, WR), F32),
            dma((H, 2, 5, 3)), dma((H, 2, 5, 3)),
            dma((H,)), dma((H,)),
            dma((H, 8)), dma((H, 8)),
            dma((H,)), dma((H,)),
            dma((3,)), dma((3,)),
            dma((H, 4, 8)), dma((H, 4, 8)),
            dma((H, 4, 2, 8)), dma((H, 4, 2, 2)), dma((H, 4, 2)),
            dma((H, 2, 8)), dma((H, 2, 8)), dma((H, 2, 8)), dma((H, 2, 8)), dma((H, 2, 8)),
            dma((H, 2)), dma((H, 2)),
            dma((H, 2)), dma((H,)),
            dma((H, 2, 5, 2)), dma((H, 2, 5, 2)),
            dma((H, 3)), dma((H, 3)),
            dma((4,)),
        ],
        compiler_params=pltpu.CompilerParams(
            collective_id=0, has_side_effects=True, vmem_limit_bytes=58 * 2**20
        ),
        cost_estimate=pl.CostEstimate(flops=9663676416, bytes_accessed=2**23, transcendentals=0),
        name="selected_inverse",
    )(anc_mask, factor.transpose(0, 2, 1), inverse_block, diag_inverse.transpose(0, 2, 1))
    return off.reshape(2, 256, 512), diag.transpose(0, 2, 1)


def solution(mesh):
    placed = (P(None, "prow"), P(None, "prow", "pcol"), P("prow", "pcol"), P(None, "prow", "pcol"))
    return jax.shard_map(
        shards,
        mesh=mesh,
        in_specs=placed,
        out_specs=(P(None, "prow", "pcol"), P(None, "prow", "pcol")),
        check_vma=False,
    )
```
